32 devices in a mesh: dp: 4 (over y, x), expert: 8 (over z, core).
Axes of the slice: x: 2, y: 2, z: 4, core: 2. Of those that a mesh axis runs over, the one named last changes fastest.
Arguments:
- tokens: bfloat16 [4096, 2048], P(('dp', 'expert')), may hold values from -6 to 6
- out_grad: bfloat16 [4096, 2048], P(('dp', 'expert')), may hold values from -6 to 6
- gate_probs: bfloat16 [4096, 4], P(('dp', 'expert')), may hold values from 0.049804688 to 0.59765625
- expert_ids: int32 [4096, 4], P(('dp', 'expert')), may hold values from 0 to 7, all different within a row; in each aligned block of 128 rows (0 to 127, 128 to 255, ...) at most 72 rows name the same one
- w_gate: bfloat16 [8, 2048, 768], P('expert'), may hold values from -0.125 to 0.125
- w_up: bfloat16 [8, 2048, 768], P('expert'), may hold values from -0.125 to 0.125
- w_down: bfloat16 [8, 768, 2048], P('expert'), may hold values from -0.21875 to 0.21875
Outputs:
- tokens_grad: bfloat16 [4096, 2048], P(('dp', 'expert'))
- probs_grad: float32 [4096, 4], P(('dp', 'expert'))
- gate_weight_grad: bfloat16 [8, 2048, 768], P('expert', None, 'dp')
- up_weight_grad: bfloat16 [8, 2048, 768], P('expert', None, 'dp')
- down_weight_grad: bfloat16 [8, 768, 2048], P('expert', 'dp')
The draws below stay inside these ranges and needn't reach their ends.
Inputs may be any that keep to these rules, and one draw needn't show every extreme that they name: `expert_ids`: each row names 4 different experts. In each aligned block of 128 rows (the rows of one device) no expert is named by more than 72 rows, a bound that some block reaches.
All inputs are finite; a program needn't handle non-finite values.
Results may differ from the reference program's by a relative error of at most 0.0057.
Values may be sent and summed in bfloat16 or wider, within the bound.
A program may use at most 192 MiB of HBM per device.

```python
import math
import jax
import jax.numpy as jnp
import numpy as np
from jax import lax

D = 2048
H = 768
TOP = 4
TOK_DEV = 128
EXPERTS = 8
TOKENS = 4096
CAP = 72
N_DP = 4
N_EXPERT = 8


def block_levels(stream_key, shape, split, smallest, largest):
    loudness = 1.0
    for axis_at, shards_of in split:
        draws = jax.random.uniform(jax.random.fold_in(jax.random.fold_in(stream_key, 6), axis_at), (shards_of,), jnp.float32, smallest / len(split), largest / len(split))
        loudness = loudness * jnp.repeat(jnp.exp(draws), shape[axis_at] // shards_of).reshape((-1,) + (1,) * (len(shape) - 1 - axis_at))
    return loudness


def deal_out(stream_key, own, number, rows, count, top, bound, slope):
    order = jax.random.permutation(stream_key, count)
    packed, usual = load_shares(count, rows * top, bound, slope, True), load_shares(count, rows * top, bound, slope, False)
    places = jnp.arange(count)

    def named(lengths, turn):
        used = int((lengths > 0).sum())
        fixed = max(1, used // 4)
        passed = fixed + (places - fixed + turn * (used - fixed)) % max(1, count - fixed)
        return jnp.zeros((count,), jnp.int32).at[order[jnp.where(places < fixed, places, passed)]].set(jnp.asarray(lengths, jnp.int32))

    lengths = jnp.where(number % 4 == 0, named(packed, number // 4), named(usual, number - number // 4 - 1))
    mixed = jax.random.permutation(jax.random.fold_in(own, 3), count)
    donor, sink = mixed[0:count // 2 * 2:2], mixed[1:count // 2 * 2:2]
    slack = jnp.minimum(lengths[donor] - 1, bound - lengths[sink]) // 2
    slack = jnp.where((donor == order[0]) | (sink == order[0]) | (lengths[sink] == 0), 0, jnp.maximum(slack, 0))
    passed = jax.random.randint(jax.random.fold_in(own, 4), (count // 2,), 0, 1 << 20) % (slack + 1)
    lengths = lengths.at[donor].add(-passed).at[sink].add(passed)
    members = jnp.searchsorted(jnp.cumsum(lengths), jnp.arange(rows * top), side="right").astype(jnp.int32)
    table = members.reshape(top, rows).T
    table = table[jax.random.permutation(jax.random.fold_in(own, 1), rows)]
    turn = jax.random.randint(jax.random.fold_in(own, 2), (rows, 1), 0, top)
    return jnp.take_along_axis(table, (jnp.arange(top)[None, :] + turn) % top, axis=1)


def load_shares(number_of, total, reach, slope, full):
    loads = [(1 << 20) // math.isqrt(grade ** slope) + 1 for grade in range(1, number_of + 1)]
    largest = reach if full else min(reach, max(-(-total // number_of), total * loads[0] // sum(loads)))
    least = 1 if total - largest >= number_of - 1 else 0
    counts, surplus = [largest] + [least] * (number_of - 1), total - largest - least * (number_of - 1)
    while surplus > 0:
        movable = [i for i in range(1, number_of) if counts[i] < largest] or [i for i in range(1, number_of) if counts[i] < reach]
        pool, remaining = sum([loads[i] for i in movable]), surplus
        for i in movable:
            addition = min(reach - counts[i], max(1, remaining * loads[i] // pool), surplus)
            counts[i] = counts[i] + addition
            surplus = surplus - addition
    return np.array(counts)


def scatter_about(own_key, extent, deviation, bound, split=(), held_as=jnp.bfloat16):
    gain = block_levels(own_key, extent, split, -0.22, 0.18) if split else 1.0
    drawn = jax.random.normal(own_key, extent, jnp.float32) * deviation * gain
    return jnp.minimum(jnp.maximum(drawn, -bound), bound).astype(held_as)


def setup_inputs(seed: int = 0) -> dict:
    arg_keys = jax.random.split(jax.random.key(seed), 8)
    tokens = scatter_about(arg_keys[0], (TOKENS, D), 1.0, 6.0, ((0, 32),))
    out_grad = scatter_about(arg_keys[1], (TOKENS, D), 1.0, 6.0, ((0, 32),))
    gate_probs = jnp.clip(jnp.exp(math.log(0.59765625) - 2.4849066 * jax.random.uniform(arg_keys[2], (TOKENS, TOP), jnp.float32) ** block_levels(arg_keys[2], (TOKENS, TOP), ((0, 32),), -0.2, 0.2)), 0.049804688, 0.59765625).astype(jnp.bfloat16)
    expert_ids_keys = jax.random.split(jax.random.fold_in(arg_keys[3], 1), TOKENS // TOK_DEV)
    expert_ids_turns = jax.random.permutation(jax.random.fold_in(arg_keys[3], 3), TOKENS // TOK_DEV)
    expert_ids = jax.vmap(lambda own, number: deal_out(jax.random.fold_in(arg_keys[3], 2), own, number, TOK_DEV, EXPERTS, TOP, CAP, 2))(expert_ids_keys, expert_ids_turns).reshape((TOKENS, TOP))
    w_gate = scatter_about(arg_keys[4], (EXPERTS, D, H), D ** -0.5, 0.125, ((0, 8),))
    w_up = scatter_about(arg_keys[5], (EXPERTS, D, H), D ** -0.5, 0.125, ((0, 8),))
    w_down = scatter_about(arg_keys[6], (EXPERTS, H, D), H ** -0.5, 0.21875, ((0, 8),))
    return dict(tokens=tokens, out_grad=out_grad, gate_probs=gate_probs, expert_ids=expert_ids, w_gate=w_gate, w_up=w_up, w_down=w_down)


def expert_work(x_slots, dy_slots, prob_slots, gate_mat, up_mat, down_mat):
    gate_pre = jnp.dot(x_slots, gate_mat, preferred_element_type=jnp.float32)
    up_pre = jnp.dot(x_slots, up_mat, preferred_element_type=jnp.float32)
    sigmoid_gate = jax.nn.sigmoid(gate_pre)
    silu_gate = gate_pre * sigmoid_gate
    hidden_act = silu_gate * up_pre
    hidden = hidden_act.astype(jnp.bfloat16)
    grad_hidden = lax.dot_general(dy_slots, down_mat, (((1,), (1,)), ((), ())), preferred_element_type=jnp.float32)
    prob_grad = jnp.sum(hidden_act * grad_hidden, axis=1)
    scaled_hidden = prob_slots[:, None] * grad_hidden
    grad_gate = (scaled_hidden * up_pre * sigmoid_gate * (1.0 + gate_pre * (1.0 - sigmoid_gate))).astype(jnp.bfloat16)
    grad_up = (scaled_hidden * silu_gate).astype(jnp.bfloat16)
    scaled_dy = (prob_slots[:, None] * dy_slots.astype(jnp.float32)).astype(jnp.bfloat16)
    row_grad = lax.dot_general(grad_gate, gate_mat, (((1,), (1,)), ((), ())), preferred_element_type=jnp.float32)
    row_grad = row_grad + lax.dot_general(grad_up, up_mat, (((1,), (1,)), ((), ())), preferred_element_type=jnp.float32)
    return hidden, grad_gate, grad_up, scaled_dy, row_grad, prob_grad


def reference(tokens, out_grad, gate_probs, expert_ids, w_gate, w_up, w_down):
    devices = N_DP * N_EXPERT
    assigns = TOK_DEV * TOP
    block_ids = expert_ids.reshape(devices, assigns)
    onehot = (block_ids[:, :, None] == jnp.arange(EXPERTS, dtype=jnp.int32)[None, None, :]).astype(jnp.int32)
    slot_rank = jnp.sum((jnp.cumsum(onehot, axis=1) - onehot) * onehot, axis=2).astype(jnp.int32)
    slot_index = jnp.arange(devices, dtype=jnp.int32)[:, None] * CAP + slot_rank
    assign_index = jnp.arange(devices * assigns, dtype=jnp.int32).reshape(devices, assigns)
    tables = jnp.full((EXPERTS, devices * CAP), TOKENS * TOP, jnp.int32).at[block_ids, slot_index].set(assign_index)
    tokens_pad = jnp.concatenate([tokens, jnp.zeros((1, D), jnp.bfloat16)], axis=0)
    grad_pad = jnp.concatenate([out_grad, jnp.zeros((1, D), jnp.bfloat16)], axis=0)
    probs_pad = jnp.concatenate([gate_probs.reshape(-1).astype(jnp.float32), jnp.zeros((1,), jnp.float32)], axis=0)

    def step(carry, inputs):
        table, gate_mat, up_mat, down_mat = inputs
        token_row = (table // TOP).astype(jnp.int32)
        x_slots = tokens_pad[token_row]
        dy_slots = grad_pad[token_row]
        prob_slots = probs_pad[table]
        hidden, grad_gate, grad_up, scaled_dy, row_grad, prob_grad = expert_work(x_slots, dy_slots, prob_slots, gate_mat, up_mat, down_mat)
        gate_term = lax.dot_general(x_slots, grad_gate, (((0,), (0,)), ((), ())), preferred_element_type=jnp.float32)
        up_term = lax.dot_general(x_slots, grad_up, (((0,), (0,)), ((), ())), preferred_element_type=jnp.float32)
        down_term = lax.dot_general(hidden, scaled_dy, (((0,), (0,)), ((), ())), preferred_element_type=jnp.float32)
        tokens_acc = carry[0].at[token_row].add(row_grad)
        probs_acc = carry[1].at[table].add(prob_grad)
        return (tokens_acc, probs_acc), (gate_term.astype(jnp.bfloat16), up_term.astype(jnp.bfloat16), down_term.astype(jnp.bfloat16))

    start = (jnp.zeros((TOKENS + 1, D), jnp.float32), jnp.zeros((TOKENS * TOP + 1,), jnp.float32))
    finals, grads = lax.scan(step, start, (tables, w_gate, w_up, w_down))
    tokens_grad = finals[0][:TOKENS].astype(jnp.bfloat16)
    probs_grad = finals[1][:TOKENS * TOP].reshape(TOKENS, TOP)
    return tokens_grad, probs_grad, grads[0], grads[1], grads[2]
```

```python
import jax
import jax.numpy as jnp
from jax import lax
from jax.sharding import PartitionSpec as P


def rows_dot(left, right):
    return lax.dot_general(
        left, right, (((1,), (1,)), ((), ())), preferred_element_type=jnp.float32
    )


def outer_rows(left, right):
    return lax.dot_general(
        left, right, (((0,), (0,)), ((), ())), preferred_element_type=jnp.float32
    )


def per_device(tokens, out_grad, gate_probs, expert_ids, w_gate, w_up, w_down):
    n_experts = lax.axis_size("expert")
    me = lax.axis_index("expert")
    tok_rows, model_width = tokens.shape
    top_k = expert_ids.shape[1]
    capacity = tok_rows * top_k * 9 // (8 * n_experts)
    slot_rows = n_experts * capacity
    group_rows = n_experts * tok_rows

    route = jnp.concatenate([expert_ids.astype(jnp.bfloat16), gate_probs], axis=1).T
    routes = lax.all_gather(route, "expert", axis=0, tiled=False)
    x_all = lax.all_gather(tokens, "expert", axis=0, tiled=True)
    dy_all = lax.all_gather(out_grad, "expert", axis=0, tiled=True)

    ids_all = routes[:, :top_k].astype(jnp.int32)
    probs_all = routes[:, top_k:].astype(jnp.float32)
    chosen = ids_all == me
    mine = jnp.any(chosen, axis=1).reshape(group_rows)
    prob_tok = jnp.sum(jnp.where(chosen, probs_all, 0.0), axis=1).reshape(group_rows)
    rank = jnp.cumsum(mine.astype(jnp.int32)) - 1
    slot_of = jnp.where(mine, rank, -1)
    hit = slot_of[None, :] == jnp.arange(slot_rows, dtype=jnp.int32)[:, None]
    pick = hit.astype(jnp.bfloat16)
    prob_slots = jnp.sum(jnp.where(hit, prob_tok[None, :], 0.0), axis=1, keepdims=True)

    gate_mat, up_mat, down_mat = w_gate[0], w_up[0], w_down[0]
    x_slots = jnp.dot(pick, x_all, preferred_element_type=jnp.float32).astype(jnp.bfloat16)
    gate_pre = jnp.dot(x_slots, gate_mat, preferred_element_type=jnp.float32)
    up_pre = jnp.dot(x_slots, up_mat, preferred_element_type=jnp.float32)
    sig = jax.nn.sigmoid(gate_pre)
    silu = gate_pre * sig
    hidden_act = silu * up_pre
    hidden = hidden_act.astype(jnp.bfloat16)

    dy_slots = jnp.dot(pick, dy_all, preferred_element_type=jnp.float32).astype(jnp.bfloat16)
    grad_hidden = rows_dot(dy_slots, down_mat)
    prob_grad = jnp.sum(hidden_act * grad_hidden, axis=1, keepdims=True)
    scaled_hidden = prob_slots * grad_hidden
    grad_gate = (scaled_hidden * up_pre * sig * (1.0 + gate_pre * (1.0 - sig))).astype(
        jnp.bfloat16
    )
    grad_up = (scaled_hidden * silu).astype(jnp.bfloat16)
    scaled_dy = (prob_slots * dy_slots.astype(jnp.float32)).astype(jnp.bfloat16)

    down_term = outer_rows(hidden, scaled_dy).astype(jnp.bfloat16)
    down_sum = lax.psum_scatter(down_term, "dp", scatter_dimension=0, tiled=True)
    gate_term = outer_rows(grad_gate, x_slots).astype(jnp.bfloat16)
    gate_sum = lax.psum_scatter(gate_term, "dp", scatter_dimension=0, tiled=True)
    up_term = outer_rows(grad_up, x_slots).astype(jnp.bfloat16)
    up_sum = lax.psum_scatter(up_term, "dp", scatter_dimension=0, tiled=True)

    row_grad = rows_dot(
        jnp.concatenate([grad_gate, grad_up], axis=1),
        jnp.concatenate([gate_mat, up_mat], axis=1),
    ).astype(jnp.bfloat16)
    part = outer_rows(pick, row_grad).astype(jnp.bfloat16)
    tokens_grad = lax.psum_scatter(part, "expert", scatter_dimension=0, tiled=True)

    prob_back = jnp.sum(jnp.where(hit, prob_grad, 0.0), axis=0)
    prob_back = prob_back.reshape(n_experts, 1, tok_rows)
    prob_part = jnp.where(chosen, prob_back, 0.0)
    probs_grad = lax.psum_scatter(prob_part, "expert", scatter_dimension=0, tiled=False).T
    return (tokens_grad, probs_grad, gate_sum.T[None], up_sum.T[None], down_sum[None])


def solution(mesh):
    in_specs = (
        P(("dp", "expert"), None),
        P(("dp", "expert"), None),
        P(("dp", "expert"), None),
        P(("dp", "expert"), None),
        P("expert", None, None),
        P("expert", None, None),
        P("expert", None, None),
    )
    out_specs = (
        P(("dp", "expert"), None),
        P(("dp", "expert"), None),
        P("expert", None, "dp"),
        P("expert", None, "dp"),
        P("expert", "dp", None),
    )
    return jax.shard_map(
        per_device, mesh=mesh, in_specs=in_specs, out_specs=out_specs, check_vma=False
    )
```

```python
import jax
import jax.numpy as jnp
from jax import lax
from jax.sharding import PartitionSpec as P


def rows_dot(left, right):
    return lax.dot_general(
        left, right, (((1,), (1,)), ((), ())), preferred_element_type=jnp.float32
    )


def outer_rows(left, right):
    return lax.dot_general(
        left, right, (((0,), (0,)), ((), ())), preferred_element_type=jnp.float32
    )


def halve(blocks, bit, axis):
    n_dp = lax.axis_size("dp")
    mine = (lax.axis_index("dp") // bit) % 2
    keep = lax.dynamic_index_in_dim(blocks, mine, axis, keepdims=False)
    give = lax.dynamic_index_in_dim(blocks, 1 - mine, axis, keepdims=False)
    got = lax.ppermute(give, "dp", [(d, d ^ bit) for d in range(n_dp)])
    return (keep.astype(jnp.float32) + got.astype(jnp.float32)).astype(jnp.bfloat16)


def dp_sum(term):
    n_dp = lax.axis_size("dp")
    if n_dp != 4:
        return lax.psum_scatter(term, "dp", scatter_dimension=0, tiled=True)
    rows, columns = term.shape
    blocks = term.reshape(2, 2, rows // 4, columns)
    left, right = blocks[..., : columns // 2], blocks[..., columns // 2 :]
    left = halve(halve(left, 1, 1), 2, 0)
    right = halve(halve(right, 2, 0), 1, 0)
    return jnp.concatenate([left, right], axis=1)


def per_device(tokens, out_grad, gate_probs, expert_ids, w_gate, w_up, w_down):
    n_experts = lax.axis_size("expert")
    me = lax.axis_index("expert")
    tok_rows, model_width = tokens.shape
    top_k = expert_ids.shape[1]
    capacity = tok_rows * top_k * 9 // (8 * n_experts)
    slot_rows = n_experts * capacity
    group_rows = n_experts * tok_rows

    route = jnp.concatenate([expert_ids.astype(jnp.bfloat16), gate_probs], axis=1).T
    routes = lax.all_gather(route, "expert", axis=0, tiled=False)
    x_all = lax.all_gather(tokens, "expert", axis=0, tiled=True)
    dy_all = lax.all_gather(out_grad, "expert", axis=0, tiled=True)

    ids_all = routes[:, :top_k].astype(jnp.int32)
    probs_all = routes[:, top_k:].astype(jnp.float32)
    chosen = ids_all == me
    mine = jnp.any(chosen, axis=1).reshape(group_rows)
    prob_tok = jnp.sum(jnp.where(chosen, probs_all, 0.0), axis=1).reshape(group_rows)
    rank = jnp.cumsum(mine.astype(jnp.int32)) - 1
    slot_of = jnp.where(mine, rank, -1)
    hit = slot_of[None, :] == jnp.arange(slot_rows, dtype=jnp.int32)[:, None]
    pick = hit.astype(jnp.bfloat16)
    prob_slots = jnp.sum(jnp.where(hit, prob_tok[None, :], 0.0), axis=1, keepdims=True)

    gate_mat, up_mat, down_mat = w_gate[0], w_up[0], w_down[0]
    x_slots = jnp.dot(pick, x_all, preferred_element_type=jnp.float32).astype(jnp.bfloat16)
    gate_pre = jnp.dot(x_slots, gate_mat, preferred_element_type=jnp.float32)
    up_pre = jnp.dot(x_slots, up_mat, preferred_element_type=jnp.float32)
    sig = jax.nn.sigmoid(gate_pre)
    silu = gate_pre * sig
    hidden_act = silu * up_pre
    hidden = hidden_act.astype(jnp.bfloat16)

    dy_slots = jnp.dot(pick, dy_all, preferred_element_type=jnp.float32).astype(jnp.bfloat16)
    grad_hidden = rows_dot(dy_slots, down_mat)
    prob_grad = jnp.sum(hidden_act * grad_hidden, axis=1, keepdims=True)
    scaled_hidden = prob_slots * grad_hidden
    grad_gate = (scaled_hidden * up_pre * sig * (1.0 + gate_pre * (1.0 - sig))).astype(
        jnp.bfloat16
    )
    grad_up = (scaled_hidden * silu).astype(jnp.bfloat16)
    scaled_dy = (prob_slots * dy_slots.astype(jnp.float32)).astype(jnp.bfloat16)

    down_sum = dp_sum(outer_rows(hidden, scaled_dy).astype(jnp.bfloat16))

    row_grad = rows_dot(
        jnp.concatenate([grad_gate, grad_up], axis=1),
        jnp.concatenate([gate_mat, up_mat], axis=1),
    ).astype(jnp.bfloat16)
    prob_high = lax.reduce_precision(prob_grad, 8, 7)
    prob_low = prob_grad - prob_high
    extra = -(-2 * n_experts // 128) * 128
    column = jnp.arange(extra, dtype=jnp.int32)[None, :]
    prob_columns = jnp.where(column == me, prob_high, 0.0) + jnp.where(
        column == me + n_experts, prob_low, 0.0
    )
    back = jnp.concatenate([row_grad, prob_columns.astype(jnp.bfloat16)], axis=1)
    part = outer_rows(pick, back).astype(jnp.bfloat16)
    total = lax.psum_scatter(part, "expert", scatter_dimension=0, tiled=True)
    tokens_grad = total[:, :model_width]
    prob_terms = total[:, model_width : model_width + 2 * n_experts].astype(jnp.float32)
    prob_experts = prob_terms[:, :n_experts] + prob_terms[:, n_experts:]
    own = expert_ids[:, :, None] == jnp.arange(n_experts, dtype=jnp.int32)[None, None, :]
    probs_grad = jnp.sum(jnp.where(own, prob_experts[:, None, :], 0.0), axis=2)

    x_late, _ = lax.optimization_barrier((x_slots, part))
    gate_sum = dp_sum(outer_rows(grad_gate, x_late).astype(jnp.bfloat16))
    up_sum = dp_sum(outer_rows(grad_up, x_late).astype(jnp.bfloat16))
    return (tokens_grad, probs_grad, gate_sum.T[None], up_sum.T[None], down_sum[None])


def solution(mesh):
    in_specs = (
        P(("dp", "expert"), None),
        P(("dp", "expert"), None),
        P(("dp", "expert"), None),
        P(("dp", "expert"), None),
        P("expert", None, None),
        P("expert", None, None),
        P("expert", None, None),
    )
    out_specs = (
        P(("dp", "expert"), None),
        P(("dp", "expert"), None),
        P("expert", None, "dp"),
        P("expert", None, "dp"),
        P("expert", "dp", None),
    )
    return jax.shard_map(
        per_device, mesh=mesh, in_specs=in_specs, out_specs=out_specs, check_vma=False
    )
```

```python
import jax
import jax.numpy as jnp
from jax import lax
from jax.sharding import PartitionSpec as P


def rows_dot(left, right):
    return lax.dot_general(
        left, right, (((1,), (1,)), ((), ())), preferred_element_type=jnp.float32
    )


def outer_rows(left, right):
    return lax.dot_general(
        left, right, (((0,), (0,)), ((), ())), preferred_element_type=jnp.float32
    )


def halve(blocks, bit, axis):
    n_dp = lax.axis_size("dp")
    mine = (lax.axis_index("dp") // bit) % 2
    keep = lax.dynamic_index_in_dim(blocks, mine, axis, keepdims=False)
    give = lax.dynamic_index_in_dim(blocks, 1 - mine, axis, keepdims=False)
    got = lax.ppermute(give, "dp", [(d, d ^ bit) for d in range(n_dp)])
    return (keep.astype(jnp.float32) + got.astype(jnp.float32)).astype(jnp.bfloat16)


def dp_sum(term):
    n_dp = lax.axis_size("dp")
    if n_dp != 4:
        return lax.psum_scatter(term, "dp", scatter_dimension=0, tiled=True)
    rows, columns = term.shape
    blocks = term.reshape(2, 2, rows // 4, columns)
    left, right = blocks[..., : columns // 2], blocks[..., columns // 2 :]
    left = halve(halve(left, 1, 1), 2, 0)
    right = halve(halve(right, 2, 0), 1, 0)
    return jnp.concatenate([left, right], axis=1)


def per_device(tokens, out_grad, gate_probs, expert_ids, w_gate, w_up, w_down):
    n_experts = lax.axis_size("expert")
    me = lax.axis_index("expert")
    tok_rows, model_width = tokens.shape
    top_k = expert_ids.shape[1]
    capacity = tok_rows * top_k * 9 // (8 * n_experts)
    slot_rows = n_experts * capacity
    group_rows = n_experts * tok_rows

    route = jnp.concatenate([expert_ids.astype(jnp.bfloat16), gate_probs], axis=1).T
    routes = lax.all_gather(route, "expert", axis=0, tiled=False)
    x_all = lax.all_gather(tokens, "expert", axis=0, tiled=True)
    dy_all = lax.all_gather(out_grad, "expert", axis=0, tiled=True)

    ids_all = routes[:, :top_k].astype(jnp.int32)
    probs_all = routes[:, top_k:].astype(jnp.float32)
    chosen = ids_all == me
    mine = jnp.any(chosen, axis=1).reshape(group_rows)
    prob_tok = jnp.sum(jnp.where(chosen, probs_all, 0.0), axis=1).reshape(group_rows)
    rank = jnp.cumsum(mine.astype(jnp.int32)) - 1
    slot_of = jnp.where(mine, rank, -1)
    hit = slot_of[None, :] == jnp.arange(slot_rows, dtype=jnp.int32)[:, None]
    pick = hit.astype(jnp.bfloat16)
    prob_slots = jnp.sum(jnp.where(hit, prob_tok[None, :], 0.0), axis=1, keepdims=True)

    gate_mat, up_mat, down_mat = w_gate[0], w_up[0], w_down[0]
    x_slots = jnp.dot(pick, x_all, preferred_element_type=jnp.float32).astype(jnp.bfloat16)
    gate_pre = jnp.dot(x_slots, gate_mat, preferred_element_type=jnp.float32)
    up_pre = jnp.dot(x_slots, up_mat, preferred_element_type=jnp.float32)
    sig = jax.nn.sigmoid(gate_pre)
    silu = gate_pre * sig
    hidden_act = silu * up_pre
    hidden = hidden_act.astype(jnp.bfloat16)

    dy_slots = jnp.dot(pick, dy_all, preferred_element_type=jnp.float32).astype(jnp.bfloat16)
    grad_hidden = rows_dot(dy_slots, down_mat)
    prob_grad = jnp.sum(hidden_act * grad_hidden, axis=1, keepdims=True)
    scaled_hidden = prob_slots * grad_hidden
    grad_gate = (scaled_hidden * up_pre * sig * (1.0 + gate_pre * (1.0 - sig))).astype(
        jnp.bfloat16
    )
    grad_up = (scaled_hidden * silu).astype(jnp.bfloat16)
    scaled_dy = (prob_slots * dy_slots.astype(jnp.float32)).astype(jnp.bfloat16)

    down_term = outer_rows(hidden, scaled_dy).astype(jnp.bfloat16)
    down_term, row_gate = lax.optimization_barrier((down_term, grad_gate))
    down_sum = dp_sum(down_term)

    row_grad = rows_dot(
        jnp.concatenate([row_gate, grad_up], axis=1),
        jnp.concatenate([gate_mat, up_mat], axis=1),
    ).astype(jnp.bfloat16)
    prob_high = lax.reduce_precision(prob_grad, 8, 7)
    prob_low = prob_grad - prob_high
    extra = -(-2 * n_experts // 128) * 128
    column = jnp.arange(extra, dtype=jnp.int32)[None, :]
    prob_columns = jnp.where(column == me, prob_high, 0.0) + jnp.where(
        column == me + n_experts, prob_low, 0.0
    )
    back = jnp.concatenate([row_grad, prob_columns.astype(jnp.bfloat16)], axis=1)
    part = outer_rows(pick, back).astype(jnp.bfloat16)
    total = lax.psum_scatter(part, "expert", scatter_dimension=0, tiled=True)
    tokens_grad = total[:, :model_width]
    prob_terms = total[:, model_width : model_width + 2 * n_experts].astype(jnp.float32)
    prob_experts = prob_terms[:, :n_experts] + prob_terms[:, n_experts:]
    own = expert_ids[:, :, None] == jnp.arange(n_experts, dtype=jnp.int32)[None, None, :]
    probs_grad = jnp.sum(jnp.where(own, prob_experts[:, None, :], 0.0), axis=2)

    x_late, _ = lax.optimization_barrier((x_slots, part))
    gate_sum = dp_sum(outer_rows(grad_gate, x_late).astype(jnp.bfloat16))
    up_sum = dp_sum(outer_rows(grad_up, x_late).astype(jnp.bfloat16))
    return (tokens_grad, probs_grad, gate_sum.T[None], up_sum.T[None], down_sum[None])


def solution(mesh):
    in_specs = (
        P(("dp", "expert"), None),
        P(("dp", "expert"), None),
        P(("dp", "expert"), None),
        P(("dp", "expert"), None),
        P("expert", None, None),
        P("expert", None, None),
        P("expert", None, None),
    )
    out_specs = (
        P(("dp", "expert"), None),
        P(("dp", "expert"), None),
        P("expert", None, "dp"),
        P("expert", None, "dp"),
        P("expert", "dp", None),
    )
    return jax.shard_map(
        per_device, mesh=mesh, in_specs=in_specs, out_specs=out_specs, check_vma=False
    )
```
